512 devices in a mesh: dp: 32 (over y, x), expert: 16 (over z, core).
Axes of the slice: x: 4, y: 8, z: 8, core: 2. Of those that a mesh axis runs over, the one named last changes fastest.
Arguments:
- hidden_in: bfloat16 [2048, 4096], P(('dp', 'expert')), may hold values from -6 to 6
- norm_gain: bfloat16 [4096], replicated, may hold values from 0.099609375 to 1.8984375
- expert_ids: int32 [2048, 8], P(('dp', 'expert')), may hold values from 0 to 63, all different within a row; in each aligned block of 64 rows (0 to 63, 64 to 127, ...) at most 16 rows name the same one
- gate_share: bfloat16 [2048, 8], P(('dp', 'expert')), may hold values from 0.049804688 to 0.25
- w_gate: bfloat16 [512, 192, 4096], P(('dp', 'expert')), may hold values from -0.09375 to 0.09375
- w_up: bfloat16 [512, 192, 4096], P(('dp', 'expert')), may hold values from -0.09375 to 0.09375
- w_down: bfloat16 [512, 192, 4096], P(('dp', 'expert')), may hold values from -0.15625 to 0.15625
Outputs:
- layer_out: bfloat16 [2048, 4096], P(('dp', 'expert'))
The draws below stay inside these ranges and needn't reach their ends.
Inputs may be any that keep to these rules, and one draw needn't show every extreme that they name: `expert_ids`: each row names 8 different experts. Among the 64 rows of one request group (aligned blocks of 64 rows), no expert is named by more than 16 rows.
All inputs are finite; a program needn't handle non-finite values.
Results may differ from the reference program's by a relative error of at most 0.01.
Values may be sent and summed in bfloat16 or wider, within the bound.
No kernel may reach another device: no remote copies, remote signals or barrier semaphores. Data moves between devices by JAX's collectives and lax.ppermute only.
A program may use at most 64 MiB of HBM per device.

```python
import math
import jax
import jax.numpy as jnp
import numpy as np
from jax import lax

D = 4096
FF = 1536
TOP = 8
EXPERTS = 64
SPLIT = 8
FF_DEV = 192
TOK_ROW = 64
TOKENS = 2048
CAP = 16
SLOTS = 512
GROUP = 1
N_DP = 32


def block_levels(key, shape, shards, low, high):
    factor_of = 1.0
    for axis_at, blocks in shards:
        steps = jax.random.uniform(jax.random.fold_in(jax.random.fold_in(key, 6), axis_at), (blocks,), jnp.float32, low / len(shards), high / len(shards))
        factor_of = factor_of * jnp.repeat(jnp.exp(steps), shape[axis_at] // blocks).reshape((-1,) + (1,) * (len(shape) - 1 - axis_at))
    return factor_of


def routed_block(own_key, own, number, rows, number_of, top, bound, skew):
    ranking = jax.random.permutation(own_key, number_of)
    packed, common = load_shares(number_of, rows * top, bound, skew, True), load_shares(number_of, rows * top, bound, skew, False)
    places = jnp.arange(number_of)

    def named(tallies, offset_by):
        used = int((tallies > 0).sum())
        fixed = max(1, used // 4)
        moved = fixed + (places - fixed + offset_by * (used - fixed)) % max(1, number_of - fixed)
        return jnp.zeros((number_of,), jnp.int32).at[ranking[jnp.where(places < fixed, places, moved)]].set(jnp.asarray(tallies, jnp.int32))

    tallies = jnp.where(number % 4 == 0, named(packed, number // 4), named(common, number - number // 4 - 1))
    mixed = jax.random.permutation(jax.random.fold_in(own, 3), number_of)
    giver, taker = mixed[0:number_of // 2 * 2:2], mixed[1:number_of // 2 * 2:2]
    slack = jnp.minimum(tallies[giver] - 1, bound - tallies[taker]) // 2
    slack = jnp.where((giver == ranking[0]) | (taker == ranking[0]) | (tallies[taker] == 0), 0, jnp.maximum(slack, 0))
    moved = jax.random.randint(jax.random.fold_in(own, 4), (number_of // 2,), 0, 1 << 20) % (slack + 1)
    tallies = tallies.at[giver].add(-moved).at[taker].add(moved)
    labels = jnp.searchsorted(jnp.cumsum(tallies), jnp.arange(rows * top), side="right").astype(jnp.int32)
    table = labels.reshape(top, rows).T
    table = table[jax.random.permutation(jax.random.fold_in(own, 1), rows)]
    offset_by = jax.random.randint(jax.random.fold_in(own, 2), (rows, 1), 0, top)
    return jnp.take_along_axis(table, (jnp.arange(top)[None, :] + offset_by) % top, axis=1)


def load_shares(number_of, total, most, skew, full):
    portions = [(1 << 20) // math.isqrt(rank ** skew) + 1 for rank in range(1, number_of + 1)]
    largest = most if full else min(most, max(-(-total // number_of), total * portions[0] // sum(portions)))
    least = 1 if total - largest >= number_of - 1 else 0
    counts, spare = [largest] + [least] * (number_of - 1), total - largest - least * (number_of - 1)
    while spare > 0:
        movable = [i for i in range(1, number_of) if counts[i] < largest] or [i for i in range(1, number_of) if counts[i] < most]
        mass, remaining = sum([portions[i] for i in movable]), spare
        for i in movable:
            more = min(most - counts[i], max(1, remaining * portions[i] // mass), spare)
            counts[i] = counts[i] + more
            spare = spare - more
    return np.array(counts)


def gaussian(rng, shape, spread, reach, pieces=(), held_as=jnp.bfloat16):
    result = spread * jax.random.normal(rng, shape, jnp.float32)
    if pieces:
        result = result * block_levels(rng, shape, pieces, -0.22, 0.18)
    return jnp.clip(result, -reach, reach).astype(held_as)


def setup_inputs(seed: int = 0) -> dict:
    splits = jax.random.split(jax.random.key(seed), 8)
    hidden_in = gaussian(splits[0], (TOKENS, D), 1.0, 6.0, ((0, 512),))
    norm_gain = jnp.clip(1.0 + 0.18 * jax.random.normal(splits[1], (D,), jnp.float32), 0.099609375, 1.8984375).astype(jnp.bfloat16)
    expert_ids_keys = jax.random.split(jax.random.fold_in(splits[2], 1), TOKENS // TOK_ROW)
    expert_ids_turns = jax.random.permutation(jax.random.fold_in(splits[2], 3), TOKENS // TOK_ROW)
    expert_ids = jax.vmap(lambda own, number: routed_block(jax.random.fold_in(splits[2], 2), own, number, TOK_ROW, EXPERTS, TOP, CAP, 1))(expert_ids_keys, expert_ids_turns).reshape((TOKENS, TOP))
    gate_share = jnp.clip(0.049804688 + 0.20019531 * jax.random.uniform(splits[3], (TOKENS, TOP), jnp.float32) ** block_levels(splits[3], (TOKENS, TOP), ((0, 512),), -0.2, 0.2), 0.049804688, 0.25).astype(jnp.bfloat16)
    w_gate = gaussian(splits[4], (SLOTS, FF_DEV, D), D ** -0.5, 0.09375, ((0, 512),))
    w_up = gaussian(splits[5], (SLOTS, FF_DEV, D), D ** -0.5, 0.09375, ((0, 512),))
    w_down = gaussian(splits[6], (SLOTS, FF_DEV, D), FF ** -0.5, 0.15625, ((0, 512),))
    return {"hidden_in": hidden_in, "norm_gain": norm_gain, "expert_ids": expert_ids, "gate_share": gate_share, "w_gate": w_gate, "w_up": w_up, "w_down": w_down}


def expert_rows(row_block, gate_w, up_w, down_w):
    row_f = row_block.astype(jnp.float32)
    gate_vals = jnp.einsum('rd,sfd->rsf', row_f, gate_w.astype(jnp.float32))
    up_vals = jnp.einsum('rd,sfd->rsf', row_f, up_w.astype(jnp.float32))
    activated = lax.optimization_barrier((jax.nn.silu(gate_vals) * up_vals).astype(jnp.bfloat16))
    projected = jnp.einsum('rsf,sfd->rsd', activated.astype(jnp.float32), down_w.astype(jnp.float32))
    grouped = lax.optimization_barrier(jnp.sum(projected.reshape(projected.shape[0], SPLIT // GROUP, GROUP, D), axis=2))
    rounded = lax.optimization_barrier(grouped.astype(jnp.bfloat16))
    return lax.optimization_barrier(jnp.sum(rounded.astype(jnp.float32), axis=1))

def reference(hidden_in, norm_gain, expert_ids, gate_share, w_gate, w_up, w_down):
    resid = hidden_in.astype(jnp.float32)
    inv_rms = lax.rsqrt(lax.optimization_barrier(jnp.mean(resid * resid, axis=1, keepdims=True)) + 1e-06)
    normed = (resid * inv_rms * norm_gain.astype(jnp.float32)[None, :]).astype(jnp.bfloat16)
    flat_ids = expert_ids.reshape(-1).astype(jnp.int32)
    onehot = (flat_ids[:, None] == jnp.arange(EXPERTS, dtype=jnp.int32)[None, :]).astype(jnp.int32)
    order_pos = lax.optimization_barrier(jnp.sum((jnp.cumsum(onehot, axis=0) - onehot) * onehot, axis=1)).astype(jnp.int32)
    per_expert = N_DP * CAP
    slot_index = (flat_ids * per_expert + order_pos).astype(jnp.int32)
    token_of = (jnp.arange(TOKENS * TOP, dtype=jnp.int32) // TOP).astype(jnp.int32)
    row_table = jnp.full((EXPERTS * per_expert,), TOKENS, dtype=jnp.int32).at[slot_index].set(token_of)
    padded = jnp.concatenate([normed, jnp.zeros((1, D), jnp.bfloat16)], axis=0)
    gate_all = w_gate.reshape(EXPERTS, SPLIT, FF_DEV, D)
    up_all = w_up.reshape(EXPERTS, SPLIT, FF_DEV, D)
    down_all = w_down.reshape(EXPERTS, SPLIT, FF_DEV, D)

    def one_expert(items):
        index_rows, gate_w, up_w, down_w = items
        return expert_rows(padded[index_rows], gate_w, up_w, down_w)
    expert_out = lax.map(one_expert, (row_table.reshape(EXPERTS, per_expert), gate_all, up_all, down_all))
    picked = expert_out.reshape(EXPERTS * per_expert, D)[slot_index].reshape(TOKENS, TOP, D)
    routed = lax.optimization_barrier(jnp.sum(picked * gate_share.astype(jnp.float32)[:, :, None], axis=1))
    return (resid + routed).astype(jnp.bfloat16)
```

```python
import functools

import jax
import jax.numpy as jnp
from jax import lax
from jax.experimental import pallas as pl
from jax.experimental.pallas import tpu as pltpu
from jax.sharding import PartitionSpec as P

EXPERTS = 64
SPLIT = 8
TOP = 8
CHUNKS = 2
VMEM = pl.BlockSpec(memory_space=pltpu.VMEM)
SMEM = pl.BlockSpec(memory_space=pltpu.SMEM)
PARAMS = pltpu.CompilerParams(vmem_limit_bytes=48 * 1024 * 1024)
NT = (((1,), (1,)), ((), ()))


def dot_nt(a, b):
    return lax.dot_general(a, b, NT, preferred_element_type=jnp.float32)


def norm_kernel(x_ref, gain_ref, meta_ref, out_ref):
    width = x_ref.shape[1]
    x = x_ref[...].astype(jnp.float32)
    inv = lax.rsqrt(jnp.mean(x * x, axis=1, keepdims=True) + 1e-06)
    out_ref[:, :width] = (x * inv * gain_ref[...].astype(jnp.float32)).astype(jnp.bfloat16)
    out_ref[:, width:] = meta_ref[...]


def pack_kernel(place_ref, row_ref, *outs):
    packed, weights = outs[:CHUNKS], outs[CHUNKS:]
    core, half = place_ref[0], place_ref[1]
    tokens = row_ref.shape[0]
    width = row_ref.shape[1] - 128
    part = width // 2
    rows = packed[0].shape[0]
    per = rows // (EXPERTS // 2)
    meta = row_ref[:, width:].astype(jnp.float32)
    lanes = lax.broadcasted_iota(jnp.int32, (tokens, EXPERTS), 1).astype(jnp.float32)
    named = jnp.zeros((tokens, EXPERTS), jnp.float32)
    share = jnp.zeros((tokens, EXPERTS), jnp.float32)
    for k in range(TOP):
        hit = meta[:, k : k + 1] == lanes
        named = jnp.where(hit, 1.0, named)
        share = jnp.where(hit, meta[:, TOP + k : TOP + k + 1], share)
    t_row = lax.broadcasted_iota(jnp.int32, (tokens, tokens), 0)
    t_col = lax.broadcasted_iota(jnp.int32, (tokens, tokens), 1)
    lower = (t_col < t_row).astype(jnp.bfloat16)
    before = jnp.dot(lower, named.astype(jnp.bfloat16), preferred_element_type=jnp.float32)
    rank = jnp.where(named > 0.0, before, -1.0).astype(jnp.bfloat16)
    slot = lax.broadcasted_iota(jnp.int32, (rows, EXPERTS), 0)
    expert = lax.broadcasted_iota(jnp.int32, (rows, EXPERTS), 1)
    pick = (expert == 2 * (slot // per) + half).astype(jnp.bfloat16)
    rank_of = dot_nt(pick, rank)
    rank_by = dot_nt(rank, pick)
    share_by = dot_nt(share.astype(jnp.bfloat16), pick)
    slot_of = (lax.broadcasted_iota(jnp.int32, (rows, tokens), 0) % per).astype(jnp.float32)
    slot_by = (lax.broadcasted_iota(jnp.int32, (tokens, rows), 1) % per).astype(jnp.float32)
    mine = row_ref[:, pl.ds(pl.multiple_of(core * part, 128), part)]
    for n in range(CHUNKS):
        first = float(n * per)
        chosen = (rank_of == slot_of + first).astype(jnp.bfloat16)
        packed[n][...] = jnp.dot(chosen, mine, preferred_element_type=jnp.float32).astype(jnp.bfloat16)
        weights[n][...] = jnp.where(rank_by == slot_by + first, share_by, 0.0).astype(jnp.bfloat16)


def up_kernel(place_ref, own_ref, other_ref, gate_ref, up_ref, down_ref, act_ref, give_ref):
    core = place_ref[0]
    part = own_ref.shape[1]
    mine = pl.ds(pl.multiple_of(core * part, 128), part)
    theirs = pl.ds(pl.multiple_of((1 - core) * part, 128), part)
    own, other = own_ref[...], other_ref[...]
    gate = dot_nt(own, gate_ref[:, mine]) + dot_nt(other, gate_ref[:, theirs])
    up = dot_nt(own, up_ref[:, mine]) + dot_nt(other, up_ref[:, theirs])
    act = (gate / (1.0 + jnp.exp(-gate)) * up).astype(jnp.bfloat16)
    act_ref[...] = act
    give_ref[...] = jnp.dot(act, down_ref[:, theirs], preferred_element_type=jnp.float32).astype(jnp.bfloat16)


def down_kernel(place_ref, act_ref, down_ref, got_ref, out_ref):
    part = got_ref.shape[1]
    mine = pl.ds(pl.multiple_of(place_ref[0] * part, 128), part)
    value = jnp.dot(act_ref[...], down_ref[:, mine], preferred_element_type=jnp.float32)
    out_ref[...] = (value + got_ref[...].astype(jnp.float32)).astype(jnp.bfloat16)


def combine_kernel(*refs):
    out_ref = refs[-1]
    total = None
    for n in range(CHUNKS):
        part = jnp.dot(refs[n][...], refs[CHUNKS + n][...], preferred_element_type=jnp.float32)
        total = part if total is None else total + part
    out_ref[...] = total.astype(jnp.bfloat16)


def final_kernel(resid_ref, got_ref, out_ref):
    tokens, part = got_ref.shape[1], got_ref.shape[2]
    for core in range(2):
        total = resid_ref[:, core * part : (core + 1) * part].astype(jnp.float32)
        for z in range(got_ref.shape[0] // 2):
            total = total + got_ref[2 * z + core].astype(jnp.float32)
        out_ref[:, core * part : (core + 1) * part] = total.astype(jnp.bfloat16)


def call(kernel, out_shape, *args, scalars=0):
    return pl.pallas_call(
        kernel,
        out_shape=out_shape,
        in_specs=[SMEM] * scalars + [VMEM] * (len(args) - scalars),
        out_specs=jax.tree.map(lambda _: VMEM, out_shape),
        compiler_params=PARAMS,
    )(*args)


def bf16(*shape):
    return jax.ShapeDtypeStruct(shape, jnp.bfloat16)


def body(hidden_in, norm_gain, expert_ids, gate_share, w_gate, w_up, w_down):
    dp_count = lax.axis_size("dp")
    col_count = lax.axis_size("expert")
    column = lax.axis_index("expert")
    tok_dev, width = hidden_in.shape
    units = w_gate.shape[1]
    tok_row = tok_dev * col_count
    part = width // 2
    per = tok_row // 4 // CHUNKS
    rows = dp_count * per
    place = jnp.stack([column % 2, column // (col_count // 2)]).astype(jnp.int32)
    partner = [(i, i ^ 1) for i in range(col_count)]
    gate_w, up_w, down_w = (w.reshape(units, width) for w in (w_gate, w_up, w_down))

    meta = jnp.concatenate([expert_ids.astype(jnp.bfloat16), gate_share], axis=1)
    meta = jnp.pad(meta, ((0, 0), (0, 128 - 2 * TOP)))
    normed = call(norm_kernel, bf16(tok_dev, width + 128), hidden_in, norm_gain.reshape(1, width), meta)
    row = lax.all_gather(normed, "expert", axis=0, tiled=True)
    outs = call(pack_kernel, [bf16(rows, part)] * CHUNKS + [bf16(tok_row, rows)] * CHUNKS, place, row, scalars=1)
    packed, weights = outs[:CHUNKS], outs[CHUNKS:]

    landed = [
        lax.all_to_all(p.reshape(dp_count, per, part), "dp", split_axis=0, concat_axis=0, tiled=True).reshape(rows, part)
        for p in packed
    ]
    returned = []
    for own in landed:
        other = lax.ppermute(own, "expert", partner)
        act, give = call(
            up_kernel, [bf16(rows, units), bf16(rows, part)], place, own, other, gate_w, up_w, down_w, scalars=1
        )
        got = lax.ppermute(give, "expert", partner)
        value = call(down_kernel, bf16(rows, part), place, act, down_w, got, scalars=1)
        back = lax.all_to_all(value.reshape(dp_count, per, part), "dp", split_axis=0, concat_axis=0, tiled=True)
        returned.append(back.reshape(rows, part))
    routed = call(combine_kernel, bf16(tok_row, part), *weights, *returned)
    shares = lax.all_to_all(
        routed.reshape(col_count, tok_dev, part), "expert", split_axis=0, concat_axis=0, tiled=True
    )
    return call(final_kernel, bf16(tok_dev, width), hidden_in, shares)


def solution(mesh):
    rows = P(("dp", "expert"), None)
    blocks = P(("dp", "expert"), None, None)
    return jax.shard_map(
        body, mesh=mesh, in_specs=(rows, P(), rows, rows, blocks, blocks, blocks), out_specs=rows, check_vma=False
    )
```

```python
import jax
import jax.numpy as jnp
from jax import lax
from jax.experimental import pallas as pl
from jax.experimental.pallas import tpu as pltpu
from jax.sharding import PartitionSpec as P

EXPERTS = 64
TOP = 8
CHUNKS = 2
META = 128
VMEM = pl.BlockSpec(memory_space=pltpu.VMEM)
HBM = pl.BlockSpec(memory_space=pltpu.HBM)
PARAMS = pltpu.CompilerParams(vmem_limit_bytes=20 * 1024 * 1024)
WHOLE = pltpu.CompilerParams(vmem_limit_bytes=62 * 1024 * 1024)
NT = (((1,), (1,)), ((), ()))


def dot_nt(a, b):
    return lax.dot_general(a, b, NT, preferred_element_type=jnp.float32)


def dot_nn(a, b):
    return jnp.dot(a, b, preferred_element_type=jnp.float32)


def norm_kernel(x_hbm, gain_hbm, ids_hbm, share_hbm, out_ref, x_ref, gain_ref, ids_ref, share_ref, sems):
    copies = [
        pltpu.make_async_copy(src, dst, sems.at[n])
        for n, (src, dst) in enumerate(
            [(x_hbm, x_ref), (gain_hbm, gain_ref), (ids_hbm, ids_ref), (share_hbm, share_ref)]
        )
    ]
    for copy in copies:
        copy.start()
    for copy in copies:
        copy.wait()
    part = x_ref.shape[1] // 2
    x = x_ref[...].astype(jnp.float32)
    inv = lax.rsqrt(jnp.mean(x * x, axis=1, keepdims=True) + 1e-06)
    normed = (x * inv * gain_ref[...].astype(jnp.float32)[None, :]).astype(jnp.bfloat16)
    ids = ids_ref[...].astype(jnp.float32)
    share = share_ref[...].astype(jnp.float32)
    lane = lax.broadcasted_iota(jnp.int32, (x.shape[0], META), 1)
    meta = jnp.zeros((x.shape[0], META), jnp.float32)
    for k in range(TOP):
        meta = jnp.where(lane == k, ids[:, k : k + 1], meta)
        meta = jnp.where(lane == TOP + k, share[:, k : k + 1], meta)
    meta = meta.astype(jnp.bfloat16)
    for j in range(out_ref.shape[0]):
        half = j % 2
        out_ref[j, :, :part] = normed[:, half * part : (half + 1) * part]
        out_ref[j, :, part:] = meta


def ranks(meta):
    tokens = meta.shape[0]
    meta = meta.astype(jnp.float32)
    lanes = lax.broadcasted_iota(jnp.int32, (tokens, EXPERTS), 1).astype(jnp.float32)
    named = jnp.zeros((tokens, EXPERTS), jnp.float32)
    share = jnp.zeros((tokens, EXPERTS), jnp.float32)
    for k in range(TOP):
        hit = meta[:, k : k + 1] == lanes
        named = jnp.where(hit, 1.0, named)
        share = jnp.where(hit, meta[:, TOP + k : TOP + k + 1], share)
    t_row = lax.broadcasted_iota(jnp.int32, (tokens, tokens), 0)
    t_col = lax.broadcasted_iota(jnp.int32, (tokens, tokens), 1)
    before = dot_nn((t_col < t_row).astype(jnp.bfloat16), named.astype(jnp.bfloat16))
    rank = jnp.where(named > 0.0, before, -1.0)
    return rank.astype(jnp.bfloat16), share.astype(jnp.bfloat16)


def picks(rows):
    per = rows // (EXPERTS // 2)
    slot = lax.broadcasted_iota(jnp.int32, (rows, EXPERTS), 0)
    expert = lax.broadcasted_iota(jnp.int32, (rows, EXPERTS), 1)
    return (expert == 2 * (slot // per) + lax.axis_index("expert") // 8).astype(jnp.bfloat16)


def pack_kernel(row_ref, quarter_ref, half_ref):
    tokens, (rows, part) = row_ref.shape[0], quarter_ref.shape
    width = half_ref.shape[1]
    per = rows // (EXPERTS // 2)
    _, b = place()
    rank, _ = ranks(row_ref[:, width:])
    rank_of = dot_nt(picks(rows), rank)
    slot = (lax.broadcasted_iota(jnp.int32, (rows, tokens), 0) % per).astype(jnp.float32)
    early = (rank_of == slot).astype(jnp.bfloat16)
    late = (rank_of == slot + float(per)).astype(jnp.bfloat16)
    quarter = row_ref[:, pl.ds(pl.multiple_of(b * part, part), part)]
    half_ref[...] = dot_nn(late, row_ref[:, :width]).astype(jnp.bfloat16)
    quarter_ref[...] = dot_nn(early, quarter).astype(jnp.bfloat16)


def weigh_kernel(row_ref, *outs):
    rank, share = ranks(row_ref[:, row_ref.shape[1] - META :])
    tokens, rows = outs[0].shape
    per = rows // (EXPERTS // 2)
    pick = picks(rows)
    rank_by, share_by = dot_nt(rank, pick), dot_nt(share, pick)
    slot = (lax.broadcasted_iota(jnp.int32, (tokens, rows), 1) % per).astype(jnp.float32)
    for n in range(CHUNKS):
        outs[n][...] = jnp.where(rank_by == slot + float(n * per), share_by, 0.0).astype(jnp.bfloat16)


def place():
    column = lax.axis_index("expert")
    return column % 2, (column // 2) % 2


def columns(ref, index, parts):
    part = ref.shape[1] // parts
    return ref[:, pl.ds(pl.multiple_of(index * part, part), part)]


def silu_mul(gate, up):
    return (gate / (1.0 + jnp.exp(-gate)) * up).astype(jnp.bfloat16)


def pair_first_kernel(own_ref, core_ref, gate_ref, up_ref, gate_out, up_out):
    c, b = place()
    own, other = own_ref[...], core_ref[...]
    mine, theirs = 2 * c + b, 2 * (1 - c) + b
    gate_out[...] = dot_nt(own, columns(gate_ref, mine, 4)) + dot_nt(other, columns(gate_ref, theirs, 4))
    up_out[...] = dot_nt(own, columns(up_ref, mine, 4)) + dot_nt(other, columns(up_ref, theirs, 4))


def pair_act_kernel(z_ref, diag_ref, gate_in, up_in, gate_ref, up_ref, down_ref, act_ref, give_ref):
    c, b = place()
    own, other = z_ref[...], diag_ref[...]
    mine, theirs = 2 * c + 1 - b, 2 * (1 - c) + 1 - b
    gate = gate_in[...] + dot_nt(own, columns(gate_ref, mine, 4)) + dot_nt(other, columns(gate_ref, theirs, 4))
    up = up_in[...] + dot_nt(own, columns(up_ref, mine, 4)) + dot_nt(other, columns(up_ref, theirs, 4))
    act = silu_mul(gate, up)
    act_ref[...] = act
    give_ref[...] = dot_nn(act, columns(down_ref, 1 - c, 2)).astype(jnp.bfloat16)


def half_first_kernel(own_ref, gate_ref, up_ref, gate_out, up_out):
    c, _ = place()
    own = own_ref[...]
    gate_out[...] = dot_nt(own, columns(gate_ref, c, 2))
    up_out[...] = dot_nt(own, columns(up_ref, c, 2))


def half_act_kernel(other_ref, gate_in, up_in, gate_ref, up_ref, down_ref, act_ref, give_ref):
    c, _ = place()
    other = other_ref[...]
    gate = gate_in[...] + dot_nt(other, columns(gate_ref, 1 - c, 2))
    up = up_in[...] + dot_nt(other, columns(up_ref, 1 - c, 2))
    act = silu_mul(gate, up)
    act_ref[...] = act
    give_ref[...] = dot_nn(act, columns(down_ref, 1 - c, 2)).astype(jnp.bfloat16)


def half_down_kernel(act_ref, down_ref, got_ref, out_ref):
    c, _ = place()
    total = dot_nn(act_ref[...], columns(down_ref, c, 2)) + got_ref[...].astype(jnp.float32)
    out_ref[...] = total.astype(jnp.bfloat16)


def pair_down_kernel(act_ref, down_ref, got_ref, mine_ref, send_ref):
    c, b = place()
    act = act_ref[...]
    send = dot_nn(act, columns(down_ref, 2 * c + 1 - b, 4)) + columns(got_ref, 1 - b, 2).astype(jnp.float32)
    send_ref[...] = send.astype(jnp.bfloat16)
    mine_ref[...] = dot_nn(act, columns(down_ref, 2 * c + b, 4)) + columns(got_ref, b, 2).astype(jnp.float32)


def add_kernel(mine_ref, got_ref, out_ref):
    out_ref[...] = (mine_ref[...] + got_ref[...].astype(jnp.float32)).astype(jnp.bfloat16)


def weighted_kernel(weight_ref, in_ref, out_ref):
    out_ref[...] = dot_nn(weight_ref[...], in_ref[...])


def combine_kernel(weight_ref, in_ref, whole_ref, out_ref):
    _, b = place()
    part = in_ref.shape[1]
    some = dot_nn(weight_ref[...], in_ref[...])
    out_ref[:, :part] = (whole_ref[:, :part] + jnp.where(b == 0, some, 0.0)).astype(jnp.bfloat16)
    out_ref[:, part:] = (whole_ref[:, part:] + jnp.where(b == 0, 0.0, some)).astype(jnp.bfloat16)


def final_kernel(resid_ref, got_ref, out_ref):
    part = got_ref.shape[2]
    for c in range(2):
        cols = slice(c * part, (c + 1) * part)
        total = resid_ref[:, cols].astype(jnp.float32)
        for j in range(c, got_ref.shape[0], 2):
            total = total + got_ref[j].astype(jnp.float32)
        out_ref[:, cols] = total.astype(jnp.bfloat16)


def call(kernel, out_shape, *args):
    return pl.pallas_call(
        kernel,
        out_shape=out_shape,
        in_specs=[VMEM] * len(args),
        out_specs=jax.tree.map(lambda _: VMEM, out_shape),
        compiler_params=PARAMS,
    )(*args)


def bf16(*shape):
    return jax.ShapeDtypeStruct(shape, jnp.bfloat16)


def f32(*shape):
    return jax.ShapeDtypeStruct(shape, jnp.float32)


def body(hidden_in, norm_gain, expert_ids, gate_share, w_gate, w_up, w_down):
    dp_count = lax.axis_size("dp")
    col_count = lax.axis_size("expert")
    tok_dev, width = hidden_in.shape
    units = w_gate.shape[1]
    tok_row = tok_dev * col_count
    half, part = width // 2, width // 4
    per = tok_row // 4 // CHUNKS
    rows = dp_count * per
    core = [(i, i ^ 1) for i in range(col_count)]
    pair = [(i, i ^ 2) for i in range(col_count)]
    gate_w, up_w, down_w = (w.reshape(units, width) for w in (w_gate, w_up, w_down))
    partial_sums = [f32(rows, units)] * 2
    activated = [bf16(rows, units), bf16(rows, half)]

    def over_dp(x):
        moved = lax.all_to_all(x.reshape(dp_count, per, x.shape[1]), "dp", split_axis=0, concat_axis=0, tiled=True)
        return moved.reshape(x.shape)

    def over_expert(x):
        return lax.all_to_all(x, "expert", split_axis=0, concat_axis=0, tiled=True)

    normed = pl.pallas_call(
        norm_kernel,
        out_shape=bf16(col_count, tok_dev, half + META),
        in_specs=[HBM] * 4,
        out_specs=VMEM,
        scratch_shapes=[
            pltpu.VMEM((tok_dev, width), jnp.bfloat16),
            pltpu.VMEM((width,), jnp.bfloat16),
            pltpu.VMEM((tok_dev, TOP), jnp.int32),
            pltpu.VMEM((tok_dev, TOP), jnp.bfloat16),
            pltpu.SemaphoreType.DMA((4,)),
        ],
        compiler_params=WHOLE,
    )(hidden_in, norm_gain, expert_ids, gate_share)
    row = over_expert(normed).reshape(tok_row, half + META)
    packed = call(pack_kernel, [bf16(rows, part), bf16(rows, half)], row)
    weights = call(weigh_kernel, [bf16(tok_row, rows)] * CHUNKS, row)

    own = over_dp(packed[0])
    from_z = lax.ppermute(own, "expert", pair)
    from_core = lax.ppermute(own, "expert", core)
    gate, up = call(pair_first_kernel, partial_sums, own, from_core, gate_w, up_w)
    from_diag = lax.ppermute(from_z, "expert", core)
    act, give = call(pair_act_kernel, activated, from_z, from_diag, gate, up, gate_w, up_w, down_w)
    second = over_dp(packed[1])
    got = lax.ppermute(give, "expert", core)
    value = call(half_down_kernel, bf16(rows, half), act, down_w, got)
    second, value = lax.optimization_barrier((second, value))
    whole = over_dp(value)

    other = lax.ppermute(second, "expert", core)
    gate, up = call(half_first_kernel, partial_sums, second, gate_w, up_w)
    act, give = call(half_act_kernel, activated, other, gate, up, gate_w, up_w, down_w)
    got = lax.ppermute(give, "expert", core)
    mine, send = call(pair_down_kernel, [f32(rows, part), bf16(rows, part)], act, down_w, got)
    value = call(add_kernel, bf16(rows, part), mine, lax.ppermute(send, "expert", pair))
    some = over_dp(value)

    whole = call(weighted_kernel, f32(tok_row, half), weights[0], whole)
    routed = call(combine_kernel, bf16(tok_row, half), weights[1], some, whole)
    shares = over_expert(routed.reshape(col_count, tok_dev, half))
    return call(final_kernel, bf16(tok_dev, width), hidden_in, shares)


def solution(mesh):
    rows = P(("dp", "expert"), None)
    blocks = P(("dp", "expert"), None, None)
    return jax.shard_map(
        body, mesh=mesh, in_specs=(rows, P(), rows, rows, blocks, blocks, blocks), out_specs=rows, check_vma=False
    )
```

```python
import jax
import jax.numpy as jnp
from jax import lax
from jax.experimental import pallas as pl
from jax.experimental.pallas import tpu as pltpu
from jax.sharding import PartitionSpec as P

EXPERTS = 64
TOP = 8
CHUNKS = 2
META = 128
VMEM = pl.BlockSpec(memory_space=pltpu.VMEM)
HBM = pl.BlockSpec(memory_space=pltpu.HBM)
PARAMS = pltpu.CompilerParams(vmem_limit_bytes=20 * 1024 * 1024)
WHOLE = pltpu.CompilerParams(vmem_limit_bytes=62 * 1024 * 1024)
NT = (((1,), (1,)), ((), ()))


def dot_nt(a, b):
    return lax.dot_general(a, b, NT, preferred_element_type=jnp.float32)


def dot_nn(a, b):
    return jnp.dot(a, b, preferred_element_type=jnp.float32)


def norm_kernel(x_hbm, gain_hbm, ids_hbm, share_hbm, out_ref, x_ref, gain_ref, ids_ref, share_ref, sems):
    copies = [
        pltpu.make_async_copy(src, dst, sems.at[n])
        for n, (src, dst) in enumerate(
            [(x_hbm, x_ref), (gain_hbm, gain_ref), (ids_hbm, ids_ref), (share_hbm, share_ref)]
        )
    ]
    for copy in copies:
        copy.start()
    for copy in copies:
        copy.wait()
    part = x_ref.shape[1] // 4
    x = x_ref[...].astype(jnp.float32)
    inv = lax.rsqrt(jnp.mean(x * x, axis=1, keepdims=True) + 1e-06)
    normed = (x * inv * gain_ref[...].astype(jnp.float32)[None, :]).astype(jnp.bfloat16)
    ids = ids_ref[...].astype(jnp.float32)
    share = share_ref[...].astype(jnp.float32)
    lane = lax.broadcasted_iota(jnp.int32, (x.shape[0], META), 1)
    meta = jnp.zeros((x.shape[0], META), jnp.float32)
    for k in range(TOP):
        meta = jnp.where(lane == k, ids[:, k : k + 1], meta)
        meta = jnp.where(lane == TOP + k, share[:, k : k + 1], meta)
    meta = meta.astype(jnp.bfloat16)
    for j in range(out_ref.shape[0]):
        q = 2 * (j % 2) + (j // 2) % 2
        out_ref[j, :, :part] = normed[:, q * part : (q + 1) * part]
        out_ref[j, :, part:] = meta


def ranks(meta):
    tokens = meta.shape[0]
    meta = meta.astype(jnp.float32)
    lanes = lax.broadcasted_iota(jnp.int32, (tokens, EXPERTS), 1).astype(jnp.float32)
    named = jnp.zeros((tokens, EXPERTS), jnp.float32)
    share = jnp.zeros((tokens, EXPERTS), jnp.float32)
    for k in range(TOP):
        hit = meta[:, k : k + 1] == lanes
        named = jnp.where(hit, 1.0, named)
        share = jnp.where(hit, meta[:, TOP + k : TOP + k + 1], share)
    t_row = lax.broadcasted_iota(jnp.int32, (tokens, tokens), 0)
    t_col = lax.broadcasted_iota(jnp.int32, (tokens, tokens), 1)
    before = dot_nn((t_col < t_row).astype(jnp.bfloat16), named.astype(jnp.bfloat16))
    rank = jnp.where(named > 0.0, before, -1.0)
    return rank.astype(jnp.bfloat16), share.astype(jnp.bfloat16)


def picks(rows):
    per = rows // (EXPERTS // 2)
    slot = lax.broadcasted_iota(jnp.int32, (rows, EXPERTS), 0)
    expert = lax.broadcasted_iota(jnp.int32, (rows, EXPERTS), 1)
    return (expert == 2 * (slot // per) + lax.axis_index("expert") // 8).astype(jnp.bfloat16)


def pack_kernel(row_ref, early_ref, late_ref, quarter_ref):
    tokens, (rows, part) = row_ref.shape[0], early_ref.shape
    per = rows // (EXPERTS // 2)
    rank, _ = ranks(row_ref[:, part:])
    rank_of = dot_nt(picks(rows), rank)
    slot = (lax.broadcasted_iota(jnp.int32, (rows, tokens), 0) % per).astype(jnp.float32)
    quarter_ref[...] = row_ref[:, :part]
    early_ref[...] = dot_nn((rank_of == slot).astype(jnp.bfloat16), row_ref[:, :part]).astype(jnp.bfloat16)
    late_ref[...] = (rank_of == slot + float(per)).astype(jnp.bfloat16)


def late_kernel(late_ref, row_ref, other_ref, out_ref):
    part = other_ref.shape[1]
    _, b = place()
    late = late_ref[...]
    own = pl.ds(pl.multiple_of(b * part, part), part)
    other = pl.ds(pl.multiple_of((1 - b) * part, part), part)
    out_ref[:, own] = dot_nn(late, row_ref[:, :part]).astype(jnp.bfloat16)
    out_ref[:, other] = dot_nn(late, other_ref[...]).astype(jnp.bfloat16)


def weigh_kernel(row_ref, *outs):
    rank, share = ranks(row_ref[:, row_ref.shape[1] - META :])
    tokens, rows = outs[0].shape
    per = rows // (EXPERTS // 2)
    pick = picks(rows)
    rank_by, share_by = dot_nt(rank, pick), dot_nt(share, pick)
    slot = (lax.broadcasted_iota(jnp.int32, (tokens, rows), 1) % per).astype(jnp.float32)
    for n in range(CHUNKS):
        outs[n][...] = jnp.where(rank_by == slot + float(n * per), share_by, 0.0).astype(jnp.bfloat16)


def place():
    column = lax.axis_index("expert")
    return column % 2, (column // 2) % 2


def columns(ref, index, parts):
    part = ref.shape[1] // parts
    return ref[:, pl.ds(pl.multiple_of(index * part, part), part)]


def silu_mul(gate, up):
    return (gate / (1.0 + jnp.exp(-gate)) * up).astype(jnp.bfloat16)


def pair_first_kernel(own_ref, core_ref, gate_ref, up_ref, gate_out, up_out):
    c, b = place()
    own, other = own_ref[...], core_ref[...]
    mine, theirs = 2 * c + b, 2 * (1 - c) + b
    gate_out[...] = dot_nt(own, columns(gate_ref, mine, 4)) + dot_nt(other, columns(gate_ref, theirs, 4))
    up_out[...] = dot_nt(own, columns(up_ref, mine, 4)) + dot_nt(other, columns(up_ref, theirs, 4))


def pair_act_kernel(z_ref, diag_ref, gate_in, up_in, gate_ref, up_ref, down_ref, act_ref, give_ref):
    c, b = place()
    own, other = z_ref[...], diag_ref[...]
    mine, theirs = 2 * c + 1 - b, 2 * (1 - c) + 1 - b
    gate = gate_in[...] + dot_nt(own, columns(gate_ref, mine, 4)) + dot_nt(other, columns(gate_ref, theirs, 4))
    up = up_in[...] + dot_nt(own, columns(up_ref, mine, 4)) + dot_nt(other, columns(up_ref, theirs, 4))
    act = silu_mul(gate, up)
    act_ref[...] = act
    give_ref[...] = dot_nn(act, columns(down_ref, 1 - c, 2)).astype(jnp.bfloat16)


def half_first_kernel(own_ref, gate_ref, up_ref, gate_out, up_out):
    c, _ = place()
    own = own_ref[...]
    gate_out[...] = dot_nt(own, columns(gate_ref, c, 2))
    up_out[...] = dot_nt(own, columns(up_ref, c, 2))


def half_act_kernel(other_ref, gate_in, up_in, gate_ref, up_ref, down_ref, act_ref, give_ref):
    c, _ = place()
    other = other_ref[...]
    gate = gate_in[...] + dot_nt(other, columns(gate_ref, 1 - c, 2))
    up = up_in[...] + dot_nt(other, columns(up_ref, 1 - c, 2))
    act = silu_mul(gate, up)
    act_ref[...] = act
    give_ref[...] = dot_nn(act, columns(down_ref, 1 - c, 2)).astype(jnp.bfloat16)


def half_down_kernel(act_ref, down_ref, got_ref, out_ref):
    c, _ = place()
    total = dot_nn(act_ref[...], columns(down_ref, c, 2)) + got_ref[...].astype(jnp.float32)
    out_ref[...] = total.astype(jnp.bfloat16)


def pair_down_kernel(act_ref, down_ref, got_ref, mine_ref, send_ref):
    c, b = place()
    act = act_ref[...]
    send = dot_nn(act, columns(down_ref, 2 * c + 1 - b, 4)) + columns(got_ref, 1 - b, 2).astype(jnp.float32)
    send_ref[...] = send.astype(jnp.bfloat16)
    mine_ref[...] = dot_nn(act, columns(down_ref, 2 * c + b, 4)) + columns(got_ref, b, 2).astype(jnp.float32)


def add_kernel(mine_ref, got_ref, out_ref):
    out_ref[...] = (mine_ref[...] + got_ref[...].astype(jnp.float32)).astype(jnp.bfloat16)


def weighted_kernel(weight_ref, in_ref, mine_ref, send_ref):
    _, b = place()
    weight = weight_ref[...]
    mine_ref[...] = dot_nn(weight, columns(in_ref, b, 2))
    send_ref[...] = dot_nn(weight, columns(in_ref, 1 - b, 2)).astype(jnp.bfloat16)


def combine_kernel(weight_ref, in_ref, mine_ref, got_ref, out_ref):
    total = dot_nn(weight_ref[...], in_ref[...]) + mine_ref[...] + got_ref[...].astype(jnp.float32)
    out_ref[...] = total.astype(jnp.bfloat16)


def final_kernel(resid_ref, got_ref, out_ref):
    part = got_ref.shape[2]
    for q in range(4):
        cols = slice(q * part, (q + 1) * part)
        total = resid_ref[:, cols].astype(jnp.float32)
        for j in range(2 * (q % 2) + q // 2, got_ref.shape[0], 4):
            total = total + got_ref[j].astype(jnp.float32)
        out_ref[:, cols] = total.astype(jnp.bfloat16)


def call(kernel, out_shape, *args):
    return pl.pallas_call(
        kernel,
        out_shape=out_shape,
        in_specs=[VMEM] * len(args),
        out_specs=jax.tree.map(lambda _: VMEM, out_shape),
        compiler_params=PARAMS,
    )(*args)


def bf16(*shape):
    return jax.ShapeDtypeStruct(shape, jnp.bfloat16)


def f32(*shape):
    return jax.ShapeDtypeStruct(shape, jnp.float32)


def body(hidden_in, norm_gain, expert_ids, gate_share, w_gate, w_up, w_down):
    dp_count = lax.axis_size("dp")
    col_count = lax.axis_size("expert")
    tok_dev, width = hidden_in.shape
    units = w_gate.shape[1]
    tok_row = tok_dev * col_count
    half, part = width // 2, width // 4
    per = tok_row // 4 // CHUNKS
    rows = dp_count * per
    core = [(i, i ^ 1) for i in range(col_count)]
    pair = [(i, i ^ 2) for i in range(col_count)]
    gate_w, up_w, down_w = (w.reshape(units, width) for w in (w_gate, w_up, w_down))
    partial_sums = [f32(rows, units)] * 2
    activated = [bf16(rows, units), bf16(rows, half)]

    def over_dp(x):
        moved = lax.all_to_all(x.reshape(dp_count, per, x.shape[1]), "dp", split_axis=0, concat_axis=0, tiled=True)
        return moved.reshape(x.shape)

    def over_expert(x):
        return lax.all_to_all(x, "expert", split_axis=0, concat_axis=0, tiled=True)

    normed = pl.pallas_call(
        norm_kernel,
        out_shape=bf16(col_count, tok_dev, part + META),
        in_specs=[HBM] * 4,
        out_specs=VMEM,
        scratch_shapes=[
            pltpu.VMEM((tok_dev, width), jnp.bfloat16),
            pltpu.VMEM((width,), jnp.bfloat16),
            pltpu.VMEM((tok_dev, TOP), jnp.int32),
            pltpu.VMEM((tok_dev, TOP), jnp.bfloat16),
            pltpu.SemaphoreType.DMA((4,)),
        ],
        compiler_params=WHOLE,
    )(hidden_in, norm_gain, expert_ids, gate_share)
    row = over_expert(normed).reshape(tok_row, part + META)
    early, late, quarter = call(pack_kernel, [bf16(rows, part), bf16(rows, tok_row), bf16(tok_row, part)], row)
    other = lax.ppermute(quarter, "expert", pair)
    packed = [early, call(late_kernel, bf16(rows, half), late, row, other)]
    weights = call(weigh_kernel, [bf16(tok_row, rows)] * CHUNKS, row)

    own, packed[1] = lax.optimization_barrier((over_dp(packed[0]), packed[1]))
    from_z = lax.ppermute(own, "expert", pair)
    from_core = lax.ppermute(own, "expert", core)
    gate, up = call(pair_first_kernel, partial_sums, own, from_core, gate_w, up_w)
    from_diag = lax.ppermute(from_z, "expert", core)
    act, give = call(pair_act_kernel, activated, from_z, from_diag, gate, up, gate_w, up_w, down_w)
    second = over_dp(packed[1])
    got = lax.ppermute(give, "expert", core)
    value = call(half_down_kernel, bf16(rows, half), act, down_w, got)
    second, value = lax.optimization_barrier((second, value))
    whole = over_dp(value)

    other = lax.ppermute(second, "expert", core)
    gate, up = call(half_first_kernel, partial_sums, second, gate_w, up_w)
    act, give = call(half_act_kernel, activated, other, gate, up, gate_w, up_w, down_w)
    got = lax.ppermute(give, "expert", core)
    mine, send = call(pair_down_kernel, [f32(rows, part), bf16(rows, part)], act, down_w, got)
    value = call(add_kernel, bf16(rows, part), mine, lax.ppermute(send, "expert", pair))
    some = over_dp(value)

    mine, send = call(weighted_kernel, [f32(tok_row, part), bf16(tok_row, part)], weights[0], whole)
    got = lax.ppermute(send, "expert", pair)
    routed = call(combine_kernel, bf16(tok_row, part), weights[1], some, mine, got)
    shares = over_expert(routed.reshape(col_count, tok_dev, part))
    return call(final_kernel, bf16(tok_dev, width), hidden_in, shares)


def solution(mesh):
    rows = P(("dp", "expert"), None)
    blocks = P(("dp", "expert"), None, None)
    return jax.shard_map(
        body, mesh=mesh, in_specs=(rows, P(), rows, rows, blocks, blocks, blocks), out_specs=rows, check_vma=False
    )
```

```python
import jax
import jax.numpy as jnp
from jax import lax
from jax.experimental import pallas as pl
from jax.experimental.pallas import tpu as pltpu
from jax.sharding import PartitionSpec as P

EXPERTS = 64
TOP = 8
META = 128
GROUP = 4
VMEM = pl.BlockSpec(memory_space=pltpu.VMEM)
ANY = pl.BlockSpec(memory_space=pl.ANY)
HBM = pl.BlockSpec(memory_space=pltpu.HBM)
PARAMS = pltpu.CompilerParams(vmem_limit_bytes=20 * 1024 * 1024)
WHOLE = pltpu.CompilerParams(vmem_limit_bytes=62 * 1024 * 1024)
NT = (((1,), (1,)), ((), ()))


def dot_nt(a, b):
    return lax.dot_general(a, b, NT, preferred_element_type=jnp.float32)


def dot_tn(a, b):
    return lax.dot_general(a, b, (((0,), (0,)), ((), ())), preferred_element_type=jnp.float32)


def dot_nn(a, b):
    return jnp.dot(a, b, preferred_element_type=jnp.float32)


def norm_kernel(x_hbm, gain_hbm, ids_hbm, share_hbm, out_ref, x_ref, gain_ref, ids_ref, share_ref, sems):
    copies = [
        pltpu.make_async_copy(src, dst, sems.at[n])
        for n, (src, dst) in enumerate(
            [(x_hbm, x_ref), (gain_hbm, gain_ref), (ids_hbm, ids_ref), (share_hbm, share_ref)]
        )
    ]
    for copy in copies:
        copy.start()
    for copy in copies:
        copy.wait()
    part = x_ref.shape[1] // 2
    x = x_ref[...].astype(jnp.float32)
    inv = lax.rsqrt(jnp.mean(x * x, axis=1, keepdims=True) + 1e-06)
    normed = (x * inv * gain_ref[...].astype(jnp.float32)[None, :]).astype(jnp.bfloat16)
    ids = ids_ref[...].astype(jnp.float32)
    share = share_ref[...].astype(jnp.float32)
    lane = lax.broadcasted_iota(jnp.int32, (x.shape[0], META), 1)
    meta = jnp.zeros((x.shape[0], META), jnp.float32)
    for k in range(TOP):
        meta = jnp.where(lane == k, ids[:, k : k + 1], meta)
        meta = jnp.where(lane == TOP + k, share[:, k : k + 1], meta)
    meta = meta.astype(jnp.bfloat16)
    for j in range(out_ref.shape[0]):
        half = j % 2
        out_ref[j, :, :part] = normed[:, half * part : (half + 1) * part]
        out_ref[j, :, part:] = meta


def ranks(meta):
    tokens = meta.shape[0]
    meta = meta.astype(jnp.float32)
    lanes = lax.broadcasted_iota(jnp.int32, (tokens, EXPERTS), 1).astype(jnp.float32)
    named = jnp.zeros((tokens, EXPERTS), jnp.float32)
    share = jnp.zeros((tokens, EXPERTS), jnp.float32)
    for k in range(TOP):
        hit = meta[:, k : k + 1] == lanes
        named = jnp.where(hit, 1.0, named)
        share = jnp.where(hit, meta[:, TOP + k : TOP + k + 1], share)
    t_row = lax.broadcasted_iota(jnp.int32, (tokens, tokens), 0)
    t_col = lax.broadcasted_iota(jnp.int32, (tokens, tokens), 1)
    before = dot_nn((t_col < t_row).astype(jnp.bfloat16), named.astype(jnp.bfloat16))
    rank = jnp.where(named > 0.0, before, -1.0)
    return rank.astype(jnp.bfloat16), share.astype(jnp.bfloat16)


def picks(rows):
    per = rows // (EXPERTS // 2)
    slot = lax.broadcasted_iota(jnp.int32, (rows, EXPERTS), 0)
    expert = lax.broadcasted_iota(jnp.int32, (rows, EXPERTS), 1)
    return (expert == 2 * (slot // per) + lax.axis_index("expert") // 8).astype(jnp.bfloat16)


def pack_kernel(row_ref, out_ref):
    tokens, (rows, part) = row_ref.shape[0], out_ref.shape
    per = rows // (EXPERTS // 2)
    rank, _ = ranks(row_ref[:, part:])
    slot = (lax.broadcasted_iota(jnp.int32, (rows, tokens), 0) % per).astype(jnp.float32)
    chosen = (dot_nt(picks(rows), rank) == slot).astype(jnp.bfloat16)
    out_ref[...] = dot_nn(chosen, row_ref[:, :part]).astype(jnp.bfloat16)


def weigh_kernel(row_ref, out_ref):
    rank, share = ranks(row_ref[:, row_ref.shape[1] - META :])
    tokens, rows = out_ref.shape
    per = rows // (EXPERTS // 2)
    pick = picks(rows)
    slot = (lax.broadcasted_iota(jnp.int32, (tokens, rows), 1) % per).astype(jnp.float32)
    out_ref[...] = jnp.where(dot_nt(rank, pick) == slot, dot_nt(share, pick), 0.0).astype(jnp.bfloat16)


def place():
    column = lax.axis_index("expert")
    return column % 2, (column // 2) % 2


def columns(ref, index, parts):
    part = ref.shape[1] // parts
    return ref[:, pl.ds(pl.multiple_of(index * part, part), part)]


def silu_mul(gate, up):
    return (gate / (1.0 + jnp.exp(-gate)) * up).astype(jnp.bfloat16)


def half_first_kernel(own_ref, gate_ref, up_ref, gate_out, up_out):
    c, _ = place()
    own = own_ref[...]
    gate_out[...] = dot_nt(columns(gate_ref, c, 2), own)
    up_out[...] = dot_nt(columns(up_ref, c, 2), own)


def half_act_kernel(other_ref, gate_in, up_in, gate_ref, up_ref, act_ref):
    c, _ = place()
    other = other_ref[...]
    gate = gate_in[...] + dot_nt(columns(gate_ref, 1 - c, 2), other)
    up = up_in[...] + dot_nt(columns(up_ref, 1 - c, 2), other)
    act_ref[...] = silu_mul(gate, up)


def own_part():
    c, b = place()
    return 2 * c + b


def give_kernel(down_ref, *outs):
    c, b = place()
    outs[0][...] = columns(down_ref, 2 * (1 - c) + b, GROUP)
    outs[1][...] = columns(down_ref, 2 * c + 1 - b, GROUP)
    outs[2][...] = columns(down_ref, 2 * (1 - c) + 1 - b, GROUP)


def touch_kernel(*refs):
    refs[-1][...] = jnp.zeros_like(refs[-1])


def down_kernel(*refs):
    acts, down_ref, others, out_ref = refs[:GROUP], refs[GROUP], refs[GROUP + 1 : 2 * GROUP], refs[-1]
    total = dot_tn(acts[0][...], columns(down_ref, own_part(), GROUP))
    for act, down in zip(acts[1:], others):
        total = total + dot_tn(act[...], down[...])
    out_ref[...] = total.astype(jnp.bfloat16)


def combine_kernel(weight_ref, in_ref, out_ref):
    out_ref[...] = dot_nn(weight_ref[...], in_ref[...]).astype(jnp.bfloat16)


def final_kernel(resid_ref, got_ref, out_ref):
    part = got_ref.shape[2]
    for q in range(GROUP):
        cols = slice(q * part, (q + 1) * part)
        total = resid_ref[:, cols].astype(jnp.float32)
        for i in range(2 * (q % 2) + q // 2, got_ref.shape[0], GROUP):
            total = total + got_ref[i].astype(jnp.float32)
        out_ref[:, cols] = total.astype(jnp.bfloat16)


def call(kernel, out_shape, *args):
    return pl.pallas_call(
        kernel,
        out_shape=out_shape,
        in_specs=[VMEM] * len(args),
        out_specs=jax.tree.map(lambda _: VMEM, out_shape),
        compiler_params=PARAMS,
    )(*args)


def bf16(*shape):
    return jax.ShapeDtypeStruct(shape, jnp.bfloat16)


def f32(*shape):
    return jax.ShapeDtypeStruct(shape, jnp.float32)


def body(hidden_in, norm_gain, expert_ids, gate_share, w_gate, w_up, w_down):
    dp_count = lax.axis_size("dp")
    col_count = lax.axis_size("expert")
    tok_dev, width = hidden_in.shape
    units = w_gate.shape[1]
    tok_row = tok_dev * col_count
    half, part = width // 2, width // GROUP
    per = tok_row // 4
    rows = dp_count * per
    def swap(x, k):
        return lax.ppermute(x, "expert", [(i, i ^ k) for i in range(col_count)])

    gate_w, up_w, down_w = (w.reshape(units, width) for w in (w_gate, w_up, w_down))
    partial_sums = [f32(units, rows)] * 2

    def over_dp(x):
        moved = lax.all_to_all(x.reshape(dp_count, per, x.shape[1]), "dp", split_axis=0, concat_axis=0, tiled=True)
        return moved.reshape(x.shape)

    def over_expert(x):
        return lax.all_to_all(x, "expert", split_axis=0, concat_axis=0, tiled=True)

    normed = pl.pallas_call(
        norm_kernel,
        out_shape=bf16(col_count, tok_dev, half + META),
        in_specs=[HBM] * 4,
        out_specs=VMEM,
        scratch_shapes=[
            pltpu.VMEM((tok_dev, width), jnp.bfloat16),
            pltpu.VMEM((width,), jnp.bfloat16),
            pltpu.VMEM((tok_dev, TOP), jnp.int32),
            pltpu.VMEM((tok_dev, TOP), jnp.bfloat16),
            pltpu.SemaphoreType.DMA((4,)),
        ],
        compiler_params=WHOLE,
    )(hidden_in, norm_gain, expert_ids, gate_share)
    row = over_expert(normed).reshape(tok_row, half + META)
    packed = call(pack_kernel, bf16(rows, half), row)
    weights = call(weigh_kernel, bf16(tok_row, rows), row)
    gives = call(give_kernel, [bf16(units, part)] * (GROUP - 1), down_w)
    downs = [swap(g, k + 1) for k, g in enumerate(gives)]
    token = pl.pallas_call(
        touch_kernel, out_shape=f32(8, 128), in_specs=[ANY] * (GROUP - 1) + [VMEM] * 2, out_specs=VMEM, compiler_params=PARAMS
    )(*downs, gate_w, up_w)

    own, token = lax.optimization_barrier((over_dp(packed), token))
    other = swap(own, 1)
    gate, up = call(half_first_kernel, partial_sums, own, gate_w, up_w)
    act = call(half_act_kernel, bf16(units, rows), other, gate, up, gate_w, up_w)
    from_z = swap(act, 2)
    acts = [act, swap(act, 1), from_z, swap(from_z, 1)]
    value = call(down_kernel, bf16(rows, part), *acts, down_w, *downs, token)
    routed = call(combine_kernel, bf16(tok_row, part), weights, over_dp(value))
    shares = over_expert(routed.reshape(col_count, tok_dev, part))
    return call(final_kernel, bf16(tok_dev, width), hidden_in, shares)


def solution(mesh):
    rows = P(("dp", "expert"), None)
    blocks = P(("dp", "expert"), None, None)
    return jax.shard_map(
        body, mesh=mesh, in_specs=(rows, P(), rows, rows, blocks, blocks, blocks), out_specs=rows, check_vma=False
    )
```

```python
import jax
import jax.numpy as jnp
from jax import lax
from jax.experimental import pallas as pl
from jax.experimental.pallas import tpu as pltpu
from jax.sharding import PartitionSpec as P

EXPERTS = 64
TOP = 8
META = 128
GROUP = 4
VMEM = pl.BlockSpec(memory_space=pltpu.VMEM)
ANY = pl.BlockSpec(memory_space=pl.ANY)
HBM = pl.BlockSpec(memory_space=pltpu.HBM)
PARAMS = pltpu.CompilerParams(vmem_limit_bytes=20 * 1024 * 1024)
WHOLE = pltpu.CompilerParams(vmem_limit_bytes=62 * 1024 * 1024)
NT = (((1,), (1,)), ((), ()))


def dot_nt(a, b):
    return lax.dot_general(a, b, NT, preferred_element_type=jnp.float32)


def dot_tn(a, b):
    return lax.dot_general(a, b, (((0,), (0,)), ((), ())), preferred_element_type=jnp.float32)


def dot_nn(a, b):
    return jnp.dot(a, b, preferred_element_type=jnp.float32)


def norm_kernel(x_hbm, gain_hbm, ids_hbm, share_hbm, out_ref, x_ref, gain_ref, ids_ref, share_ref, sems):
    copies = [
        pltpu.make_async_copy(src, dst, sems.at[n])
        for n, (src, dst) in enumerate(
            [(x_hbm, x_ref), (gain_hbm, gain_ref), (ids_hbm, ids_ref), (share_hbm, share_ref)]
        )
    ]
    for copy in copies:
        copy.start()
    for copy in copies:
        copy.wait()
    part = x_ref.shape[1] // 2
    x = x_ref[...].astype(jnp.float32)
    inv = lax.rsqrt(jnp.mean(x * x, axis=1, keepdims=True) + 1e-06)
    normed = (x * inv * gain_ref[...].astype(jnp.float32)[None, :]).astype(jnp.bfloat16)
    ids = ids_ref[...].astype(jnp.float32)
    share = share_ref[...].astype(jnp.float32)
    lane = lax.broadcasted_iota(jnp.int32, (x.shape[0], META), 1)
    meta = jnp.zeros((x.shape[0], META), jnp.float32)
    for k in range(TOP):
        meta = jnp.where(lane == k, ids[:, k : k + 1], meta)
        meta = jnp.where(lane == TOP + k, share[:, k : k + 1], meta)
    meta = meta.astype(jnp.bfloat16)
    for j in range(out_ref.shape[0]):
        half = j % 2
        out_ref[j, :, :part] = normed[:, half * part : (half + 1) * part]
        out_ref[j, :, part:] = meta


def ranks(meta):
    tokens = meta.shape[0]
    meta = meta.astype(jnp.float32)
    lanes = lax.broadcasted_iota(jnp.int32, (tokens, EXPERTS), 1).astype(jnp.float32)
    named = jnp.zeros((tokens, EXPERTS), jnp.float32)
    share = jnp.zeros((tokens, EXPERTS), jnp.float32)
    for k in range(TOP):
        hit = meta[:, k : k + 1] == lanes
        named = jnp.where(hit, 1.0, named)
        share = jnp.where(hit, meta[:, TOP + k : TOP + k + 1], share)
    t_row = lax.broadcasted_iota(jnp.int32, (tokens, tokens), 0)
    t_col = lax.broadcasted_iota(jnp.int32, (tokens, tokens), 1)
    before = dot_nn((t_col < t_row).astype(jnp.bfloat16), named.astype(jnp.bfloat16))
    rank = jnp.where(named > 0.0, before, -1.0)
    return rank.astype(jnp.bfloat16), share.astype(jnp.bfloat16)


def picks(rows):
    per = rows // (EXPERTS // 2)
    slot = lax.broadcasted_iota(jnp.int32, (rows, EXPERTS), 0)
    expert = lax.broadcasted_iota(jnp.int32, (rows, EXPERTS), 1)
    return (expert == 2 * (slot // per) + lax.axis_index("expert") // 8).astype(jnp.bfloat16)


def pack_kernel(row_ref, out_ref):
    tokens, (rows, part) = row_ref.shape[0], out_ref.shape
    per = rows // (EXPERTS // 2)
    rank, _ = ranks(row_ref[:, part:])
    slot = (lax.broadcasted_iota(jnp.int32, (rows, tokens), 0) % per).astype(jnp.float32)
    chosen = (dot_nt(picks(rows), rank) == slot).astype(jnp.bfloat16)
    out_ref[...] = dot_nn(chosen, row_ref[:, :part]).astype(jnp.bfloat16)


def weigh_kernel(row_ref, out_ref):
    rank, share = ranks(row_ref[:, row_ref.shape[1] - META :])
    tokens, rows = out_ref.shape
    per = rows // (EXPERTS // 2)
    pick = picks(rows)
    slot = (lax.broadcasted_iota(jnp.int32, (tokens, rows), 1) % per).astype(jnp.float32)
    out_ref[...] = jnp.where(dot_nt(rank, pick) == slot, dot_nt(share, pick), 0.0).astype(jnp.bfloat16)


def place():
    column = lax.axis_index("expert")
    return column % 2, (column // 2) % 2


def columns(ref, index, parts):
    part = ref.shape[1] // parts
    return ref[:, pl.ds(pl.multiple_of(index * part, part), part)]


def silu_mul(gate, up):
    return (gate / (1.0 + jnp.exp(-gate)) * up).astype(jnp.bfloat16)


def half_first_kernel(own_ref, gate_ref, up_ref, gate_out, up_out):
    c, _ = place()
    own = own_ref[...]
    gate_out[...] = dot_nt(columns(gate_ref, c, 2), own)
    up_out[...] = dot_nt(columns(up_ref, c, 2), own)


def half_act_kernel(other_ref, gate_in, up_in, gate_ref, up_ref, act_ref):
    c, _ = place()
    other = other_ref[...]
    units = gate_ref.shape[0]
    both = jnp.concatenate([columns(gate_ref, 1 - c, 2), columns(up_ref, 1 - c, 2)], axis=0)
    both = dot_nt(both, other)
    act_ref[...] = silu_mul(gate_in[...] + both[:units], up_in[...] + both[units:])


def own_part():
    c, b = place()
    return 2 * c + b


def give_kernel(down_ref, *outs):
    c, b = place()
    outs[0][...] = columns(down_ref, 2 * (1 - c) + b, GROUP)
    outs[1][...] = columns(down_ref, 2 * c + 1 - b, GROUP)
    outs[2][...] = columns(down_ref, 2 * (1 - c) + 1 - b, GROUP)


def touch_kernel(*refs):
    refs[-1][...] = jnp.zeros_like(refs[-1])


def down_kernel(*refs):
    acts, down_ref, others, out_ref = refs[:GROUP], refs[GROUP], refs[GROUP + 1 : 2 * GROUP], refs[-1]
    downs = [columns(down_ref, own_part(), GROUP)] + [down[...] for down in others]
    act = jnp.concatenate([act[...] for act in acts], axis=0)
    out_ref[...] = dot_tn(act, jnp.concatenate(downs, axis=0)).astype(jnp.bfloat16)


def combine_kernel(weight_ref, in_ref, out_ref):
    out_ref[...] = dot_nn(weight_ref[...], in_ref[...]).astype(jnp.bfloat16)


def final_kernel(resid_ref, got_ref, out_ref):
    part = got_ref.shape[2]
    for q in range(GROUP):
        cols = slice(q * part, (q + 1) * part)
        total = resid_ref[:, cols].astype(jnp.float32)
        for i in range(2 * (q % 2) + q // 2, got_ref.shape[0], GROUP):
            total = total + got_ref[i].astype(jnp.float32)
        out_ref[:, cols] = total.astype(jnp.bfloat16)


def call(kernel, out_shape, *args):
    return pl.pallas_call(
        kernel,
        out_shape=out_shape,
        in_specs=[VMEM] * len(args),
        out_specs=jax.tree.map(lambda _: VMEM, out_shape),
        compiler_params=PARAMS,
    )(*args)


def bf16(*shape):
    return jax.ShapeDtypeStruct(shape, jnp.bfloat16)


def f32(*shape):
    return jax.ShapeDtypeStruct(shape, jnp.float32)


def body(hidden_in, norm_gain, expert_ids, gate_share, w_gate, w_up, w_down):
    dp_count = lax.axis_size("dp")
    col_count = lax.axis_size("expert")
    tok_dev, width = hidden_in.shape
    units = w_gate.shape[1]
    tok_row = tok_dev * col_count
    half, part = width // 2, width // GROUP
    per = tok_row // 4
    rows = dp_count * per
    def swap(x, k):
        return lax.ppermute(x, "expert", [(i, i ^ k) for i in range(col_count)])

    gate_w, up_w, down_w = (w.reshape(units, width) for w in (w_gate, w_up, w_down))
    partial_sums = [f32(units, rows)] * 2

    def over_dp(x):
        moved = lax.all_to_all(x.reshape(dp_count, per, x.shape[1]), "dp", split_axis=0, concat_axis=0, tiled=True)
        return moved.reshape(x.shape)

    def over_expert(x):
        return lax.all_to_all(x, "expert", split_axis=0, concat_axis=0, tiled=True)

    normed = pl.pallas_call(
        norm_kernel,
        out_shape=bf16(col_count, tok_dev, half + META),
        in_specs=[HBM] * 4,
        out_specs=VMEM,
        scratch_shapes=[
            pltpu.VMEM((tok_dev, width), jnp.bfloat16),
            pltpu.VMEM((width,), jnp.bfloat16),
            pltpu.VMEM((tok_dev, TOP), jnp.int32),
            pltpu.VMEM((tok_dev, TOP), jnp.bfloat16),
            pltpu.SemaphoreType.DMA((4,)),
        ],
        compiler_params=WHOLE,
    )(hidden_in, norm_gain, expert_ids, gate_share)
    row = over_expert(normed).reshape(tok_row, half + META)
    packed = call(pack_kernel, bf16(rows, half), row)
    weights = call(weigh_kernel, bf16(tok_row, rows), row)
    gives = call(give_kernel, [bf16(units, part)] * (GROUP - 1), down_w)
    downs = [swap(g, k + 1) for k, g in enumerate(gives)]
    token = pl.pallas_call(
        touch_kernel, out_shape=f32(8, 128), in_specs=[ANY] * (GROUP - 1) + [VMEM] * 2, out_specs=VMEM, compiler_params=PARAMS
    )(*downs, gate_w, up_w)

    own, token = lax.optimization_barrier((over_dp(packed), token))
    other = swap(own, 1)
    gate, up = call(half_first_kernel, partial_sums, own, gate_w, up_w)
    act = call(half_act_kernel, bf16(units, rows), other, gate, up, gate_w, up_w)
    from_z = swap(act, 2)
    acts = [act, swap(act, 1), from_z, swap(from_z, 1)]
    value = call(down_kernel, bf16(rows, part), *acts, down_w, *downs, token)
    routed = call(combine_kernel, bf16(tok_row, part), weights, over_dp(value))
    shares = over_expert(routed.reshape(col_count, tok_dev, part))
    return call(final_kernel, bf16(tok_dev, width), hidden_in, shares)


def solution(mesh):
    rows = P(("dp", "expert"), None)
    blocks = P(("dp", "expert"), None, None)
    return jax.shard_map(
        body, mesh=mesh, in_specs=(rows, P(), rows, rows, blocks, blocks, blocks), out_specs=rows, check_vma=False
    )
```

```python
import jax
import jax.numpy as jnp
from jax import lax
from jax.experimental import pallas as pl
from jax.experimental.pallas import tpu as pltpu
from jax.sharding import PartitionSpec as P

EXPERTS = 64
TOP = 8
META = 128
GROUP = 4
VMEM = pl.BlockSpec(memory_space=pltpu.VMEM)
ANY = pl.BlockSpec(memory_space=pl.ANY)
HBM = pl.BlockSpec(memory_space=pltpu.HBM)
PARAMS = pltpu.CompilerParams(vmem_limit_bytes=20 * 1024 * 1024)
WHOLE = pltpu.CompilerParams(vmem_limit_bytes=62 * 1024 * 1024)
NT = (((1,), (1,)), ((), ()))


def dot_nt(a, b):
    return lax.dot_general(a, b, NT, preferred_element_type=jnp.float32)


def dot_tn(a, b):
    return lax.dot_general(a, b, (((0,), (0,)), ((), ())), preferred_element_type=jnp.float32)


def dot_nn(a, b):
    return jnp.dot(a, b, preferred_element_type=jnp.float32)


def norm_kernel(x_hbm, gain_hbm, ids_hbm, share_hbm, out_ref, x_ref, gain_ref, ids_ref, share_ref, sems):
    copies = [
        pltpu.make_async_copy(src, dst, sems.at[n])
        for n, (src, dst) in enumerate(
            [(x_hbm, x_ref), (gain_hbm, gain_ref), (ids_hbm, ids_ref), (share_hbm, share_ref)]
        )
    ]
    for copy in copies:
        copy.start()
    for copy in copies:
        copy.wait()
    part = x_ref.shape[1] // 2
    x = x_ref[...].astype(jnp.float32)
    inv = lax.rsqrt(jnp.mean(x * x, axis=1, keepdims=True) + 1e-06)
    normed = (x * inv * gain_ref[...].astype(jnp.float32)[None, :]).astype(jnp.bfloat16)
    ids = ids_ref[...].astype(jnp.float32)
    share = share_ref[...].astype(jnp.float32)
    lane = lax.broadcasted_iota(jnp.int32, (x.shape[0], META), 1)
    meta = jnp.zeros((x.shape[0], META), jnp.float32)
    for k in range(TOP):
        meta = jnp.where(lane == k, ids[:, k : k + 1], meta)
        meta = jnp.where(lane == TOP + k, share[:, k : k + 1], meta)
    meta = meta.astype(jnp.bfloat16)
    for j in range(out_ref.shape[0]):
        half = j % 2
        out_ref[j, :, :part] = normed[:, half * part : (half + 1) * part]
        out_ref[j, :, part:] = meta


def ranks(meta):
    tokens = meta.shape[0]
    meta = meta.astype(jnp.float32)
    lanes = lax.broadcasted_iota(jnp.int32, (tokens, EXPERTS), 1).astype(jnp.float32)
    named = jnp.zeros((tokens, EXPERTS), jnp.float32)
    share = jnp.zeros((tokens, EXPERTS), jnp.float32)
    for k in range(TOP):
        hit = meta[:, k : k + 1] == lanes
        named = jnp.where(hit, 1.0, named)
        share = jnp.where(hit, meta[:, TOP + k : TOP + k + 1], share)
    t_row = lax.broadcasted_iota(jnp.int32, (tokens, tokens), 0)
    t_col = lax.broadcasted_iota(jnp.int32, (tokens, tokens), 1)
    before = dot_nn((t_col < t_row).astype(jnp.bfloat16), named.astype(jnp.bfloat16))
    rank = jnp.where(named > 0.0, before, -1.0)
    return rank.astype(jnp.bfloat16), share.astype(jnp.bfloat16)


def picks(rows):
    per = rows // (EXPERTS // 2)
    slot = lax.broadcasted_iota(jnp.int32, (rows, EXPERTS), 0)
    expert = lax.broadcasted_iota(jnp.int32, (rows, EXPERTS), 1)
    return (expert == 2 * (slot // per) + lax.axis_index("expert") // 8).astype(jnp.bfloat16)


def pack_kernel(row_ref, out_ref):
    tokens, (rows, part) = row_ref.shape[0], out_ref.shape
    per = rows // (EXPERTS // 2)
    rank, _ = ranks(row_ref[:, part:])
    slot = (lax.broadcasted_iota(jnp.int32, (rows, tokens), 0) % per).astype(jnp.float32)
    chosen = (dot_nt(picks(rows), rank) == slot).astype(jnp.bfloat16)
    out_ref[...] = dot_nn(chosen, row_ref[:, :part]).astype(jnp.bfloat16)


def weigh_kernel(row_ref, out_ref):
    rank, share = ranks(row_ref[:, row_ref.shape[1] - META :])
    tokens, rows = out_ref.shape
    per = rows // (EXPERTS // 2)
    pick = picks(rows)
    slot = (lax.broadcasted_iota(jnp.int32, (tokens, rows), 1) % per).astype(jnp.float32)
    out_ref[...] = jnp.where(dot_nt(rank, pick) == slot, dot_nt(share, pick), 0.0).astype(jnp.bfloat16)


def place():
    column = lax.axis_index("expert")
    return column % 2, (column // 2) % 2


def columns(ref, index, parts):
    part = ref.shape[1] // parts
    return ref[:, pl.ds(pl.multiple_of(index * part, part), part)]


def silu_mul(gate, up):
    return (gate / (1.0 + jnp.exp(-gate)) * up).astype(jnp.bfloat16)


def half_first_kernel(own_ref, gate_ref, up_ref, gate_out, up_out):
    c, _ = place()
    own = own_ref[...]
    gate_out[...] = dot_nt(columns(gate_ref, c, 2), own)
    up_out[...] = dot_nt(columns(up_ref, c, 2), own)


def half_act_kernel(other_ref, gate_in, up_in, gate_ref, up_ref, act_ref):
    c, _ = place()
    other = other_ref[...]
    units = gate_ref.shape[0]
    both = jnp.concatenate([columns(gate_ref, 1 - c, 2), columns(up_ref, 1 - c, 2)], axis=0)
    both = dot_nt(both, other)
    act_ref[...] = silu_mul(gate_in[...] + both[:units], up_in[...] + both[units:])


def own_part():
    c, b = place()
    return 2 * c + b


def give_kernel(down_ref, *outs):
    c, b = place()
    outs[0][...] = columns(down_ref, 2 * (1 - c) + b, GROUP)
    outs[1][...] = columns(down_ref, 2 * c + 1 - b, GROUP)
    outs[2][...] = columns(down_ref, 2 * (1 - c) + 1 - b, GROUP)


def touch_kernel(*refs):
    refs[-1][...] = jnp.zeros_like(refs[-1])


def near_kernel(own_act, core_act, down_ref, core_ref, token_ref, out_ref):
    act = jnp.concatenate([own_act[...], core_act[...]], axis=0)
    out_ref[...] = dot_tn(act, jnp.concatenate([columns(down_ref, own_part(), GROUP), core_ref[...]], axis=0))


def far_kernel(near_ref, z_act, diag_act, z_ref, diag_ref, out_ref):
    act = jnp.concatenate([z_act[...], diag_act[...]], axis=0)
    total = near_ref[...] + dot_tn(act, jnp.concatenate([z_ref[...], diag_ref[...]], axis=0))
    out_ref[...] = total.astype(jnp.bfloat16)


def combine_kernel(weight_ref, in_ref, out_ref):
    out_ref[...] = dot_nn(weight_ref[...], in_ref[...]).astype(jnp.bfloat16)


def final_kernel(resid_ref, got_ref, out_ref):
    part = got_ref.shape[2]
    for q in range(GROUP):
        cols = slice(q * part, (q + 1) * part)
        total = resid_ref[:, cols].astype(jnp.float32)
        for i in range(2 * (q % 2) + q // 2, got_ref.shape[0], GROUP):
            total = total + got_ref[i].astype(jnp.float32)
        out_ref[:, cols] = total.astype(jnp.bfloat16)


def call(kernel, out_shape, *args):
    return pl.pallas_call(
        kernel,
        out_shape=out_shape,
        in_specs=[VMEM] * len(args),
        out_specs=jax.tree.map(lambda _: VMEM, out_shape),
        compiler_params=PARAMS,
    )(*args)


def bf16(*shape):
    return jax.ShapeDtypeStruct(shape, jnp.bfloat16)


def f32(*shape):
    return jax.ShapeDtypeStruct(shape, jnp.float32)


def body(hidden_in, norm_gain, expert_ids, gate_share, w_gate, w_up, w_down):
    dp_count = lax.axis_size("dp")
    col_count = lax.axis_size("expert")
    tok_dev, width = hidden_in.shape
    units = w_gate.shape[1]
    tok_row = tok_dev * col_count
    half, part = width // 2, width // GROUP
    per = tok_row // 4
    rows = dp_count * per
    def swap(x, k):
        return lax.ppermute(x, "expert", [(i, i ^ k) for i in range(col_count)])

    gate_w, up_w, down_w = (w.reshape(units, width) for w in (w_gate, w_up, w_down))
    partial_sums = [f32(units, rows)] * 2

    def over_dp(x):
        moved = lax.all_to_all(x.reshape(dp_count, per, x.shape[1]), "dp", split_axis=0, concat_axis=0, tiled=True)
        return moved.reshape(x.shape)

    def over_expert(x):
        return lax.all_to_all(x, "expert", split_axis=0, concat_axis=0, tiled=True)

    normed = pl.pallas_call(
        norm_kernel,
        out_shape=bf16(col_count, tok_dev, half + META),
        in_specs=[HBM] * 4,
        out_specs=VMEM,
        scratch_shapes=[
            pltpu.VMEM((tok_dev, width), jnp.bfloat16),
            pltpu.VMEM((width,), jnp.bfloat16),
            pltpu.VMEM((tok_dev, TOP), jnp.int32),
            pltpu.VMEM((tok_dev, TOP), jnp.bfloat16),
            pltpu.SemaphoreType.DMA((4,)),
        ],
        compiler_params=WHOLE,
    )(hidden_in, norm_gain, expert_ids, gate_share)
    row = over_expert(normed).reshape(tok_row, half + META)
    packed = call(pack_kernel, bf16(rows, half), row)
    weights = call(weigh_kernel, bf16(tok_row, rows), row)
    gives = call(give_kernel, [bf16(units, part)] * (GROUP - 1), down_w)
    downs = [swap(g, k + 1) for k, g in enumerate(gives)]
    token = pl.pallas_call(
        touch_kernel, out_shape=f32(8, 128), in_specs=[ANY] * (GROUP - 1) + [VMEM] * 2, out_specs=VMEM, compiler_params=PARAMS
    )(*downs, gate_w, up_w)

    own, token = lax.optimization_barrier((over_dp(packed), token))
    other = swap(own, 1)
    gate, up = call(half_first_kernel, partial_sums, own, gate_w, up_w)
    act = call(half_act_kernel, bf16(units, rows), other, gate, up, gate_w, up_w)
    from_z = swap(act, 2)
    acts = [act, swap(act, 1), from_z, swap(from_z, 1)]
    near = call(near_kernel, f32(rows, part), acts[0], acts[1], down_w, downs[0], token)
    value = call(far_kernel, bf16(rows, part), near, acts[2], acts[3], downs[1], downs[2])
    routed = call(combine_kernel, bf16(tok_row, part), weights, over_dp(value))
    shares = over_expert(routed.reshape(col_count, tok_dev, part))
    return call(final_kernel, bf16(tok_dev, width), hidden_in, shares)


def solution(mesh):
    rows = P(("dp", "expert"), None)
    blocks = P(("dp", "expert"), None, None)
    return jax.shard_map(
        body, mesh=mesh, in_specs=(rows, P(), rows, rows, blocks, blocks, blocks), out_specs=rows, check_vma=False
    )
```

```python
import jax
import jax.numpy as jnp
from jax import lax
from jax.experimental import pallas as pl
from jax.experimental.pallas import tpu as pltpu
from jax.sharding import PartitionSpec as P

EXPERTS = 64
TOP = 8
META = 128
GROUP = 4
VMEM = pl.BlockSpec(memory_space=pltpu.VMEM)
ANY = pl.BlockSpec(memory_space=pl.ANY)
HBM = pl.BlockSpec(memory_space=pltpu.HBM)
PARAMS = pltpu.CompilerParams(vmem_limit_bytes=20 * 1024 * 1024)
WHOLE = pltpu.CompilerParams(vmem_limit_bytes=62 * 1024 * 1024)
NT = (((1,), (1,)), ((), ()))


def dot_nt(a, b):
    return lax.dot_general(a, b, NT, preferred_element_type=jnp.float32)


def dot_tn(a, b):
    return lax.dot_general(a, b, (((0,), (0,)), ((), ())), preferred_element_type=jnp.float32)


def dot_nn(a, b):
    return jnp.dot(a, b, preferred_element_type=jnp.float32)


def norm_kernel(x_hbm, gain_hbm, ids_hbm, share_hbm, out_ref, x_ref, gain_ref, ids_ref, share_ref, sems):
    copies = [
        pltpu.make_async_copy(src, dst, sems.at[n])
        for n, (src, dst) in enumerate(
            [(x_hbm, x_ref), (gain_hbm, gain_ref), (ids_hbm, ids_ref), (share_hbm, share_ref)]
        )
    ]
    for copy in copies:
        copy.start()
    for copy in copies[2:]:
        copy.wait()
    part = x_ref.shape[1] // 2
    ids = ids_ref[...].astype(jnp.float32)
    share = share_ref[...].astype(jnp.float32)
    lane = lax.broadcasted_iota(jnp.int32, (x_ref.shape[0], META), 1)
    meta = jnp.zeros((x_ref.shape[0], META), jnp.float32)
    for k in range(TOP):
        meta = jnp.where(lane == k, ids[:, k : k + 1], meta)
        meta = jnp.where(lane == TOP + k, share[:, k : k + 1], meta)
    meta = meta.astype(jnp.bfloat16)
    for j in range(out_ref.shape[0]):
        out_ref[j, :, part:] = meta
    for copy in copies[:2]:
        copy.wait()
    x = x_ref[...].astype(jnp.float32)
    inv = lax.rsqrt(jnp.mean(x * x, axis=1, keepdims=True) + 1e-06)
    normed = (x * inv * gain_ref[...].astype(jnp.float32)[None, :]).astype(jnp.bfloat16)
    for j in range(out_ref.shape[0]):
        half = j % 2
        out_ref[j, :, :part] = normed[:, half * part : (half + 1) * part]


def ranks(meta):
    tokens = meta.shape[0]
    meta = meta.astype(jnp.float32)
    lanes = lax.broadcasted_iota(jnp.int32, (tokens, EXPERTS), 1).astype(jnp.float32)
    named = jnp.zeros((tokens, EXPERTS), jnp.float32)
    share = jnp.zeros((tokens, EXPERTS), jnp.float32)
    for k in range(TOP):
        hit = meta[:, k : k + 1] == lanes
        named = jnp.where(hit, 1.0, named)
        share = jnp.where(hit, meta[:, TOP + k : TOP + k + 1], share)
    t_row = lax.broadcasted_iota(jnp.int32, (tokens, tokens), 0)
    t_col = lax.broadcasted_iota(jnp.int32, (tokens, tokens), 1)
    before = dot_nn((t_col < t_row).astype(jnp.bfloat16), named.astype(jnp.bfloat16))
    rank = jnp.where(named > 0.0, before, -1.0)
    return rank.astype(jnp.bfloat16), share.astype(jnp.bfloat16)


def picks(rows):
    per = rows // (EXPERTS // 2)
    slot = lax.broadcasted_iota(jnp.int32, (rows, EXPERTS), 0)
    expert = lax.broadcasted_iota(jnp.int32, (rows, EXPERTS), 1)
    return (expert == 2 * (slot // per) + lax.axis_index("expert") // 8).astype(jnp.bfloat16)


def pack_kernel(row_ref, out_ref):
    tokens, (rows, part) = row_ref.shape[0], out_ref.shape
    per = rows // (EXPERTS // 2)
    rank, _ = ranks(row_ref[:, part:])
    slot = (lax.broadcasted_iota(jnp.int32, (rows, tokens), 0) % per).astype(jnp.float32)
    chosen = (dot_nt(picks(rows), rank) == slot).astype(jnp.bfloat16)
    out_ref[...] = dot_nn(chosen, row_ref[:, :part]).astype(jnp.bfloat16)


def weigh_kernel(row_ref, out_ref):
    rank, share = ranks(row_ref[:, row_ref.shape[1] - META :])
    tokens, rows = out_ref.shape
    per = rows // (EXPERTS // 2)
    pick = picks(rows)
    slot = (lax.broadcasted_iota(jnp.int32, (tokens, rows), 1) % per).astype(jnp.float32)
    out_ref[...] = jnp.where(dot_nt(rank, pick) == slot, dot_nt(share, pick), 0.0).astype(jnp.bfloat16)


def place():
    column = lax.axis_index("expert")
    return column % 2, (column // 2) % 2


def columns(ref, index, parts):
    part = ref.shape[1] // parts
    return ref[:, pl.ds(pl.multiple_of(index * part, part), part)]


def silu_mul(gate, up):
    return (gate / (1.0 + jnp.exp(-gate)) * up).astype(jnp.bfloat16)


def half_first_kernel(own_ref, gate_ref, up_ref, gate_out, up_out):
    c, _ = place()
    own = own_ref[...]
    gate_out[...] = dot_nt(columns(gate_ref, c, 2), own)
    up_out[...] = dot_nt(columns(up_ref, c, 2), own)


def half_act_kernel(other_ref, gate_in, up_in, gate_ref, up_ref, act_ref):
    c, _ = place()
    other = other_ref[...]
    units = gate_ref.shape[0]
    both = jnp.concatenate([columns(gate_ref, 1 - c, 2), columns(up_ref, 1 - c, 2)], axis=0)
    both = dot_nt(both, other)
    act_ref[...] = silu_mul(gate_in[...] + both[:units], up_in[...] + both[units:])


def own_part():
    c, b = place()
    return 2 * c + b


def give_kernel(down_ref, *outs):
    c, b = place()
    outs[0][...] = columns(down_ref, 2 * (1 - c) + b, GROUP)
    outs[1][...] = columns(down_ref, 2 * c + 1 - b, GROUP)
    outs[2][...] = columns(down_ref, 2 * (1 - c) + 1 - b, GROUP)


def touch_kernel(*refs):
    refs[-1][...] = jnp.zeros_like(refs[-1])


def near_kernel(own_act, core_act, down_ref, core_ref, token_ref, out_ref):
    act = jnp.concatenate([own_act[...], core_act[...]], axis=0)
    out_ref[...] = dot_tn(act, jnp.concatenate([columns(down_ref, own_part(), GROUP), core_ref[...]], axis=0))


def far_kernel(near_ref, z_act, diag_act, z_ref, diag_ref, out_ref):
    act = jnp.concatenate([z_act[...], diag_act[...]], axis=0)
    total = near_ref[...] + dot_tn(act, jnp.concatenate([z_ref[...], diag_ref[...]], axis=0))
    out_ref[...] = total.astype(jnp.bfloat16)


def combine_kernel(weight_ref, in_ref, out_ref):
    out_ref[...] = dot_nn(weight_ref[...], in_ref[...]).astype(jnp.bfloat16)


def final_kernel(resid_ref, got_ref, out_ref):
    part = got_ref.shape[2]
    for q in range(GROUP):
        cols = slice(q * part, (q + 1) * part)
        total = resid_ref[:, cols].astype(jnp.float32)
        for i in range(2 * (q % 2) + q // 2, got_ref.shape[0], GROUP):
            total = total + got_ref[i].astype(jnp.float32)
        out_ref[:, cols] = total.astype(jnp.bfloat16)


def call(kernel, out_shape, *args):
    return pl.pallas_call(
        kernel,
        out_shape=out_shape,
        in_specs=[VMEM] * len(args),
        out_specs=jax.tree.map(lambda _: VMEM, out_shape),
        compiler_params=PARAMS,
    )(*args)


def bf16(*shape):
    return jax.ShapeDtypeStruct(shape, jnp.bfloat16)


def f32(*shape):
    return jax.ShapeDtypeStruct(shape, jnp.float32)


def body(hidden_in, norm_gain, expert_ids, gate_share, w_gate, w_up, w_down):
    dp_count = lax.axis_size("dp")
    col_count = lax.axis_size("expert")
    tok_dev, width = hidden_in.shape
    units = w_gate.shape[1]
    tok_row = tok_dev * col_count
    half, part = width // 2, width // GROUP
    per = tok_row // 4
    rows = dp_count * per
    def swap(x, k):
        return lax.ppermute(x, "expert", [(i, i ^ k) for i in range(col_count)])

    gate_w, up_w, down_w = (w.reshape(units, width) for w in (w_gate, w_up, w_down))
    partial_sums = [f32(units, rows)] * 2

    def over_dp(x):
        moved = lax.all_to_all(x.reshape(dp_count, per, x.shape[1]), "dp", split_axis=0, concat_axis=0, tiled=True)
        return moved.reshape(x.shape)

    def over_expert(x):
        return lax.all_to_all(x, "expert", split_axis=0, concat_axis=0, tiled=True)

    normed = pl.pallas_call(
        norm_kernel,
        out_shape=bf16(col_count, tok_dev, half + META),
        in_specs=[HBM] * 4,
        out_specs=VMEM,
        scratch_shapes=[
            pltpu.VMEM((tok_dev, width), jnp.bfloat16),
            pltpu.VMEM((width,), jnp.bfloat16),
            pltpu.VMEM((tok_dev, TOP), jnp.int32),
            pltpu.VMEM((tok_dev, TOP), jnp.bfloat16),
            pltpu.SemaphoreType.DMA((4,)),
        ],
        compiler_params=WHOLE,
    )(hidden_in, norm_gain, expert_ids, gate_share)
    row = over_expert(normed).reshape(tok_row, half + META)
    packed = call(pack_kernel, bf16(rows, half), row)
    weights = call(weigh_kernel, bf16(tok_row, rows), row)
    gives = call(give_kernel, [bf16(units, part)] * (GROUP - 1), down_w)
    downs = [swap(g, k + 1) for k, g in enumerate(gives)]
    token = pl.pallas_call(
        touch_kernel, out_shape=f32(8, 128), in_specs=[ANY] * (GROUP - 1) + [VMEM] * 2, out_specs=VMEM, compiler_params=PARAMS
    )(*downs, gate_w, up_w)

    own, token = lax.optimization_barrier((over_dp(packed), token))
    other = swap(own, 1)
    gate, up = call(half_first_kernel, partial_sums, own, gate_w, up_w)
    act = call(half_act_kernel, bf16(units, rows), other, gate, up, gate_w, up_w)
    from_z = swap(act, 2)
    acts = [act, swap(act, 1), from_z, swap(from_z, 1)]
    near = call(near_kernel, f32(rows, part), acts[0], acts[1], down_w, downs[0], token)
    value = call(far_kernel, bf16(rows, part), near, acts[2], acts[3], downs[1], downs[2])
    routed = call(combine_kernel, bf16(tok_row, part), weights, over_dp(value))
    shares = over_expert(routed.reshape(col_count, tok_dev, part))
    return call(final_kernel, bf16(tok_dev, width), hidden_in, shares)


def solution(mesh):
    rows = P(("dp", "expert"), None)
    blocks = P(("dp", "expert"), None, None)
    return jax.shard_map(
        body, mesh=mesh, in_specs=(rows, P(), rows, rows, blocks, blocks, blocks), out_specs=rows, check_vma=False
    )
```
